256 devices in a mesh: rep: 8 (over z_hi, core), fsdp: 32 (over y, z_lo, x).
Axes of the slice: x: 4, y: 4, z: 8 (z_hi: 4, z_lo: 2; z = z_hi * 2 + z_lo), core: 2. Of those that a mesh axis runs over, the one named last changes fastest.
Arguments:
- tokens: bfloat16 [8, 8192, 4608], P('rep', 'fsdp'), may hold values from -800 to 800
- norm_scale: float32 [8, 4608], P('rep'), may hold values from 0.25 to 1.75
- value_weight: bfloat16 [8, 4608, 1024], P('rep', 'fsdp'), may hold values from -0.09375 to 0.09375
- cotangent: bfloat16 [8, 8192, 1024], P('rep', 'fsdp'), may hold values from -6 to 6
- replica_weights: bfloat16 [8, 2, 4608, 1024], P('rep', None, 'fsdp'), may hold values from -6 to 6
- base: float32 [2, 4608, 1024], P(None, 'fsdp'), may hold values from -6 to 6
- momentum: float32 [2, 4608, 1024], P(None, 'fsdp'), may hold values from -4 to 4
- fragment: int32 [576], P('fsdp'), may hold values from 0 to 1
Outputs:
- values: bfloat16 [8, 8192, 1024], P('rep', 'fsdp')
- input_grad: bfloat16 [8, 8192, 4608], P('rep', 'fsdp')
- weight_grad: float32 [8, 4608, 1024], P('rep', 'fsdp')
- scale_grad: float32 [8, 4608], P('rep', 'fsdp')
- new_base: float32 [4608, 1024], P('fsdp')
- new_momentum: float32 [4608, 1024], P('fsdp')
The draws below stay inside these ranges and needn't reach their ends.
All inputs are finite; a program needn't handle non-finite values.
Results may differ from the reference program's by a relative error of at most 0.0049.
Values may be sent and summed in bfloat16 or wider, within the bound.
No kernel may reach another device: no remote copies, remote signals or barrier semaphores. Data moves between devices by JAX's collectives and lax.ppermute only.
A program may use at most 128 MiB of HBM per device.

```python
import math
import jax
import jax.numpy as jnp
from jax import lax

D = 4608
HV = 1024
TOKENS = 8192
REPLICAS = 8
FRAGS = 2
FC = 1024
N_REP = 8


def draw_tokens(key, part):
    key = jax.random.fold_in(key, 11)
    first, second, third = jax.random.split(key, 3)
    shape = (REPLICAS, TOKENS, D)
    drawn = jnp.clip(jax.random.normal(first, shape), -6.0, 6.0)
    rows = jnp.exp(jax.random.uniform(second, (REPLICAS, TOKENS, 1)) * math.log(10.0))
    mixed = drawn * rows
    columns = jnp.exp(jax.random.uniform(third, (1, 1, D)) * math.log(10.0))
    return (mixed * columns).astype(jnp.float32).astype(jnp.bfloat16)


def with_ends(array, key, low, top_value):
    index_at = [jax.random.randint(jax.random.fold_in(key, axis), (), 0, length) for axis, length in enumerate(array.shape)]
    main_axis = array.shape.index(max(array.shape))
    neighbour = index_at[:main_axis] + [(index_at[main_axis] + 1) % array.shape[main_axis]] + index_at[main_axis + 1:]
    return array.at[tuple(index_at)].set(low).at[tuple(neighbour)].set(top_value)


def level_of(rng, extent, cuts, low, largest):
    gain = 1.0
    for dim, shards_of in cuts:
        heights = jax.random.uniform(jax.random.fold_in(jax.random.fold_in(rng, 6), dim), (shards_of,), jnp.float32, low / len(cuts), largest / len(cuts))
        gain = gain * jnp.repeat(jnp.exp(heights), extent[dim] // shards_of).reshape((-1,) + (1,) * (len(extent) - 1 - dim))
    return gain


def gaussian(own_key, extent, deviation, limit, pieces=(), dtype=jnp.bfloat16):
    drawn = deviation * jax.random.normal(own_key, extent, jnp.float32)
    if pieces:
        drawn = drawn * level_of(own_key, extent, pieces, -0.22, 0.18)
    return jnp.clip(drawn, -limit, limit).astype(dtype)


def setup_inputs(seed: int = 0) -> dict:
    keys = jax.random.split(jax.random.key(seed), 9)
    return {
        "tokens": draw_tokens(jax.random.fold_in(keys[8], 71), 0),
        "norm_scale": jnp.clip(1.0 + 0.15 * jax.random.normal(keys[1], (REPLICAS, D), jnp.float32), 0.25, 1.75),
        "value_weight": gaussian(keys[2], (REPLICAS, D, HV), D ** -0.5, 0.09375, ((0, 8), (1, 32))),
        "cotangent": gaussian(keys[3], (REPLICAS, TOKENS, HV), 1.0, 6.0, ((0, 8), (1, 32))),
        "replica_weights": gaussian(keys[4], (REPLICAS, FRAGS, D, FC), 1.0, 6.0, ((0, 8), (2, 32))),
        "base": gaussian(keys[5], (FRAGS, D, FC), 1.0, 6.0, ((1, 32),), jnp.float32),
        "momentum": gaussian(keys[6], (FRAGS, D, FC), 0.5, 4.0, ((1, 32),), jnp.float32),
        "fragment": with_ends(jax.random.randint(keys[7], (D // 8,), 0, FRAGS), jax.random.fold_in(keys[7], 1), 0, FRAGS - 1).astype(jnp.int32),
    }


def inner_step(tokens_one, scale_one, weight_one, cot_one):
    inputs = tokens_one.astype(jnp.float32)
    inverse = lax.rsqrt(lax.optimization_barrier(jnp.mean(inputs * inputs, axis=-1, keepdims=True)) + 1e-06)
    normed = (inputs * inverse * scale_one).astype(jnp.bfloat16)
    values = jnp.dot(normed, weight_one, preferred_element_type=jnp.float32).astype(jnp.bfloat16)
    back = lax.dot_general(cot_one, weight_one, (((1,), (1,)), ((), ())), preferred_element_type=jnp.float32)
    scaled_back = back * scale_one
    input_grad = (inverse * (scaled_back - inputs * (inverse * inverse) * lax.optimization_barrier(jnp.mean(scaled_back * inputs, axis=-1, keepdims=True)))).astype(jnp.bfloat16)
    weight_sum = lax.dot_general(normed, cot_one, (((0,), (0,)), ((), ())), preferred_element_type=jnp.float32)
    scale_sum = lax.optimization_barrier(jnp.sum(back * inputs * inverse, axis=0))
    factor = 1.0 / math.sqrt(TOKENS)
    return (values, input_grad, weight_sum * factor, scale_sum * factor)

def pick_rows(stack, row_frag):
    result = stack[0]
    for index in range(1, stack.shape[0]):
        result = jnp.where(row_frag[:, None] == index, stack[index], result)
    return result

def reference(tokens, norm_scale, value_weight, cotangent, replica_weights, base, momentum, fragment):
    values_all, input_all, weight_all, scale_all = ([], [], [], [])
    for replica in range(N_REP):
        values, input_grad, weight_grad, scale_grad = inner_step(tokens[replica], norm_scale[replica], value_weight[replica], cotangent[replica])
        values_all.append(values)
        input_all.append(input_grad)
        weight_all.append(weight_grad)
        scale_all.append(scale_grad)
    row_frag = jnp.repeat(fragment.astype(jnp.int32), 8)
    base_now = pick_rows(base, row_frag)
    moment = pick_rows(momentum, row_frag)
    pseudo_all = []
    for replica in range(N_REP):
        weights_now = pick_rows(replica_weights[replica], row_frag).astype(jnp.float32)
        pseudo_all.append((weights_now - base_now).astype(jnp.bfloat16).astype(jnp.float32))
    delta = sum(pseudo_all) / N_REP
    new_momentum = 0.9 * moment + delta
    new_base = base_now + 0.7 * (delta + 0.9 * new_momentum)
    return (jnp.stack(values_all), jnp.stack(input_all), jnp.stack(weight_all), jnp.stack(scale_all), new_base, new_momentum)
```

```python
import functools
import math

import jax
import jax.numpy as jnp
from jax import lax
from jax.experimental import pallas as pl
from jax.experimental.pallas import tpu as pltpu
from jax.sharding import PartitionSpec as P

D = 4608
HV = 1024
ROWS = 144
HALF = D // 2
TOK = 256
NX, NY, NZ = 4, 4, 2
F32, BF16 = jnp.float32, jnp.bfloat16


def fsdp_perm(move):
    pairs = []
    for y in range(NY):
        for z in range(NZ):
            for x in range(NX):
                a, b, c = move(y, z, x)
                pairs.append(((y * NZ + z) * NX + x, (a % NY * NZ + b % NZ) * NX + c % NX))
    return pairs


def after(v, *others):
    return lax.optimization_barrier((v, *others))[0]


def send_x(v, d):
    return lax.ppermute(v, "fsdp", fsdp_perm(lambda y, z, x: (y, z, x + d)))


def send_y(v, d):
    return lax.ppermute(v, "fsdp", fsdp_perm(lambda y, z, x: (y + d, z, x)))


def send_z(v):
    return lax.ppermute(v, "fsdp", fsdp_perm(lambda y, z, x: (y, z + 1, x)))


def send_core(v):
    return lax.ppermute(v, "rep", [(i, i ^ 1) for i in range(8)])


def send_zhi(v, d):
    return lax.ppermute(v, "rep", [(2 * h + c, (h + d) % 4 * 2 + c) for h in range(4) for c in range(2)])


def norm_kernel(where_ref, tok_ref, scale_ref, keep_ref, send_ref, turned):
    y, z, x = where_ref[0], where_ref[1], where_ref[2]
    total = jnp.zeros((TOK, 128), F32)
    for k in range(D // 128):
        part = tok_ref[:, k * 128 : (k + 1) * 128].astype(F32)
        total = total + part * part
    inverse = lax.rsqrt(jnp.sum(total, axis=1, keepdims=True) * (1.0 / D) + 1e-06)
    for k in range(D // 128):
        cols = slice(k * 128, (k + 1) * 128)
        part = tok_ref[:, cols].astype(F32) * inverse * scale_ref[:, cols]
        turned[cols, :] = part.T.astype(BF16)
    for dy in range(NY):
        for dx in range(NX):
            at = slice((dy * NX + dx) * ROWS, (dy * NX + dx + 1) * ROWS)
            row, col = lax.rem(y + dy, NY), lax.rem(x + dx, NX)
            for out, side in ((keep_ref, z), (send_ref, 1 - z)):
                start = pl.multiple_of(((row * NZ + side) * NX + col) * ROWS, 16)
                out[at, :] = turned[pl.ds(start, ROWS), :]


def norm_turned(where, tokens, scale):
    vmem = pl.BlockSpec(memory_space=pltpu.VMEM)
    return pl.pallas_call(
        norm_kernel,
        out_shape=[
            jax.ShapeDtypeStruct((HALF, TOK), BF16),
            jax.ShapeDtypeStruct((HALF, TOK), BF16),
        ],
        in_specs=[pl.BlockSpec(memory_space=pltpu.SMEM), vmem, vmem],
        out_specs=[vmem] * 2,
        scratch_shapes=[pltpu.VMEM((D, TOK), BF16)],
        compiler_params=pltpu.CompilerParams(vmem_limit_bytes=32 << 20),
        cost_estimate=pl.CostEstimate(flops=8 * TOK * D, bytes_accessed=16 << 20, transcendentals=256),
        name="norm",
    )(where, tokens, scale)


def grad_kernel(keep_ref, got_ref, cot_ref, other_ref, low_ref, high_ref):
    for out, cols in ((low_ref, slice(0, HV // 2)), (high_ref, slice(HV // 2, HV))):
        part = jnp.dot(keep_ref[...], cot_ref[:, cols], preferred_element_type=F32)
        part = part + jnp.dot(got_ref[...], other_ref[:, cols], preferred_element_type=F32)
        out[...] = part.astype(BF16)


def grad_terms(keep, got, cot, other):
    tile = 288
    rows = pl.BlockSpec((tile, TOK), lambda i: (i, 0))
    whole = pl.BlockSpec((TOK, HV), lambda i: (0, 0))
    out = pl.BlockSpec((tile, HV // 2), lambda i: (i, 0))
    return pl.pallas_call(
        grad_kernel,
        grid=(HALF // tile,),
        out_shape=[jax.ShapeDtypeStruct((HALF, HV // 2), BF16)] * 2,
        in_specs=[rows, rows, whole, whole],
        out_specs=[out, out],
        compiler_params=pltpu.CompilerParams(vmem_limit_bytes=32 << 20),
        cost_estimate=pl.CostEstimate(
            flops=2 * HALF * 2 * TOK * HV, bytes_accessed=10 << 20, transcendentals=0
        ),
        name="weight_terms",
    )(keep, got, cot, other)


PIECES = ((0, (0, 1, 2, 3)), (3, (0, 1, 2, 3)), (1, (0, 1, 2, 3)), (2, (0, 1)), (2, (2, 3)))
N_PIECES = 2 * len(PIECES)


def model_kernel(*refs):
    where_ref, tok_ref, scale_ref, cot_ref = refs[:4]
    pieces = refs[4 : 4 + N_PIECES]
    val_ref, grad_ref = refs[4 + N_PIECES : 6 + N_PIECES]
    whole, normed, back, sems = refs[6 + N_PIECES :]
    y, z, x = where_ref[0], where_ref[1], where_ref[2]
    copies = []
    for half in range(2):
        for n, (ring, line) in enumerate(PIECES):
            ref = pieces[half * len(PIECES) + n]
            for i, d in enumerate(line):
                for side in range(2):
                    if half == 0:
                        row, col = lax.rem(y + ring, NY), lax.rem(x + d, NX)
                    else:
                        row, col = lax.rem(y + d, NY), lax.rem(x + ring, NX)
                    zc = z if side == 0 else 1 - z
                    at = pl.multiple_of(((row * NZ + zc) * NX + col) * ROWS, 16)
                    copy = pltpu.make_async_copy(
                        ref.at[i, side],
                        whole.at[pl.ds(at, ROWS), pl.ds(half * 512, 512)],
                        sems.at[len(copies)],
                    )
                    copy.start()
                    copies.append(copy)
    total = jnp.zeros((TOK, 128), F32)
    for k in range(D // 128):
        part = tok_ref[:, k * 128 : (k + 1) * 128].astype(F32)
        total = total + part * part
    inverse = lax.rsqrt(jnp.sum(total, axis=1, keepdims=True) * (1.0 / D) + 1e-06)
    for k in range(D // 256):
        cols = slice(k * 256, (k + 1) * 256)
        part = tok_ref[:, cols].astype(F32) * inverse * scale_ref[:, cols]
        normed[:, cols] = part.astype(BF16)
    for copy in copies:
        copy.wait()

    def project(i, _):
        cols = pl.ds(pl.multiple_of(i * 256, 256), 256)
        val_ref[:, cols] = jnp.dot(normed[...], whole[:, cols], preferred_element_type=F32).astype(BF16)
        return 0

    lax.fori_loop(0, HV // 256, project, 0)

    def pull(i, sums):
        at = pl.ds(pl.multiple_of(i * 256, 256), 256)
        term = lax.dot_general(
            cot_ref[...], whole[at, :], (((1,), (1,)), ((), ())), preferred_element_type=F32
        )
        toks = tok_ref[:, at].astype(F32)
        back[:, at] = term
        mixed = term * scale_ref[:, at] * toks
        return sums + mixed[:, :128] + mixed[:, 128:]

    sums = lax.fori_loop(0, D // 256, pull, jnp.zeros((TOK, 128), F32))
    mean = jnp.sum(sums, axis=1, keepdims=True) * (1.0 / D)
    lean = inverse * inverse * mean

    def finish(i, _):
        at = pl.ds(pl.multiple_of(i * 256, 256), 256)
        grad = inverse * (back[:, at] * scale_ref[:, at] - tok_ref[:, at].astype(F32) * lean)
        grad_ref[:, at] = grad.astype(BF16)
        return 0

    lax.fori_loop(0, D // 256, finish, 0)


def model_step(where, tokens, scale, cot, pieces):
    vmem = pl.BlockSpec(memory_space=pltpu.VMEM)
    return pl.pallas_call(
        model_kernel,
        out_shape=[
            jax.ShapeDtypeStruct((TOK, HV), BF16),
            jax.ShapeDtypeStruct((TOK, D), BF16),
        ],
        in_specs=[pl.BlockSpec(memory_space=pltpu.SMEM), vmem, vmem, vmem]
        + [pl.BlockSpec(memory_space=pl.ANY)] * N_PIECES,
        out_specs=[vmem, vmem],
        scratch_shapes=[
            pltpu.VMEM((D, HV), BF16),
            pltpu.VMEM((TOK, D), BF16),
            pltpu.VMEM((TOK, D), F32),
            pltpu.SemaphoreType.DMA((64,)),
        ],
        compiler_params=pltpu.CompilerParams(vmem_limit_bytes=48 << 20),
        cost_estimate=pl.CostEstimate(
            flops=4 * TOK * D * HV, bytes_accessed=32 << 20, transcendentals=256
        ),
        name="model_step",
    )(where, tokens, scale, cot, *pieces)


def gather_half(pair, first, second):
    near = jnp.stack([pair, first(pair, -1), first(pair, 2), first(pair, 1)])
    left, right = second(near, 1), second(near, -1)
    return [near, left, right, second(left[:2], 1), second(right[2:], -1)]


def ring_sum(blocks, send):
    n = blocks[0].shape[0] // 2
    to_far, back_far = send(blocks[2][:n], 1), send(blocks[2][n:], -1)
    up = jnp.concatenate([(blocks[1][:n].astype(F32) + to_far.astype(F32)).astype(BF16), blocks[1][n:]])
    down = jnp.concatenate([blocks[3][:n], (blocks[3][n:].astype(F32) + back_far.astype(F32)).astype(BF16)])
    return blocks[0].astype(F32) + send(up, 1).astype(F32) + send(down, -1).astype(F32)


def direct_sum(blocks, send):
    return (
        blocks[0].astype(F32)
        + send(blocks[1].astype(BF16), 1).astype(F32)
        + send(blocks[3].astype(BF16), -1).astype(F32)
        + send(blocks[2].astype(BF16), 2).astype(F32)
    )


def scatter_sum_half(terms, second_first, first):
    return direct_sum(list(ring_sum([terms[d] for d in range(4)], second_first)), first)


def pick(stack, row_frag):
    return jnp.where(row_frag[:, None] == 1, stack[1], stack[0])


def outer_sync(replica_weights, base, momentum, fragment, wait):
    row_frag = jnp.repeat(fragment, 8)
    base_now = pick(base, row_frag)
    moment = pick(momentum, row_frag)
    pseudo = (pick(replica_weights[0], row_frag).astype(F32) - base_now).astype(BF16)
    everyone = lax.all_gather(after(pseudo, wait), "rep", axis=0)
    delta = jnp.sum(everyone.astype(F32), axis=0) / everyone.shape[0]
    new_momentum = 0.9 * moment + delta
    new_base = base_now + 0.7 * (delta + 0.9 * new_momentum)
    return new_base, new_momentum


def per_device(
    tokens, norm_scale, value_weight, cotangent, replica_weights, base, momentum, fragment
):
    tokens, weight, cot = tokens[0], value_weight[0], cotangent[0]
    me = lax.axis_index("fsdp")
    where = jnp.stack([me // (NZ * NX), me // NX % NZ, me % NX]).astype(jnp.int32)
    other_weight = send_z(weight)
    keep, give = norm_turned(where, tokens, norm_scale)
    partner_cot = send_z(after(cot, other_weight, give))
    got = send_z(after(give, partner_cot))
    pieces = []
    for half in range(2):
        order = (send_x, send_y) if half == 0 else (send_y, send_x)
        cols = slice(half * 512, half * 512 + 512)
        pieces += gather_half(jnp.stack([weight[:, cols], other_weight[:, cols]]), *order)
    low, high = grad_terms(keep, got, cot, partner_cot)
    low = low.reshape(NY, NX, ROWS, HV // 2)
    high = high.reshape(NY, NX, ROWS, HV // 2).swapaxes(0, 1)
    factor = 1.0 / math.sqrt(TOK * NX * NY * NZ)
    weight_grad = jnp.concatenate(
        [scatter_sum_half(low, send_y, send_x), scatter_sum_half(high, send_x, send_y)], axis=1
    ) * factor
    mine = lax.dynamic_slice_in_dim(norm_scale[0], me * ROWS, ROWS)
    scale_grad = jnp.sum(weight.astype(F32) * weight_grad, axis=1) / mine
    values, input_grad = model_step(where, tokens, norm_scale, cot, pieces)
    new_base, new_momentum = outer_sync(replica_weights, base, momentum, fragment, got)
    return (
        values[None],
        input_grad[None],
        weight_grad[None],
        scale_grad[None],
        new_base,
        new_momentum,
    )


def solution(mesh):
    in_specs = (
        P("rep", "fsdp", None),
        P("rep", None),
        P("rep", "fsdp", None),
        P("rep", "fsdp", None),
        P("rep", None, "fsdp", None),
        P(None, "fsdp", None),
        P(None, "fsdp", None),
        P("fsdp"),
    )
    out_specs = (
        P("rep", "fsdp", None),
        P("rep", "fsdp", None),
        P("rep", "fsdp", None),
        P("rep", "fsdp"),
        P("fsdp", None),
        P("fsdp", None),
    )
    return jax.shard_map(
        per_device, mesh=mesh, in_specs=in_specs, out_specs=out_specs, check_vma=False
    )
```

```python
import functools
import math

import jax
import jax.numpy as jnp
from jax import lax
from jax.experimental import pallas as pl
from jax.experimental.pallas import tpu as pltpu
from jax.sharding import PartitionSpec as P

D = 4608
HV = 1024
ROWS = 144
HALF = D // 2
TOK = 256
NX, NY, NZ = 4, 4, 2
F32, BF16 = jnp.float32, jnp.bfloat16


def fsdp_perm(move):
    pairs = []
    for y in range(NY):
        for z in range(NZ):
            for x in range(NX):
                a, b, c = move(y, z, x)
                pairs.append(((y * NZ + z) * NX + x, (a % NY * NZ + b % NZ) * NX + c % NX))
    return pairs


def after(v, *others):
    return lax.optimization_barrier((v, *others))[0]


def send_x(v, d):
    return lax.ppermute(v, "fsdp", fsdp_perm(lambda y, z, x: (y, z, x + d)))


def send_y(v, d):
    return lax.ppermute(v, "fsdp", fsdp_perm(lambda y, z, x: (y + d, z, x)))


def send_z(v):
    return lax.ppermute(v, "fsdp", fsdp_perm(lambda y, z, x: (y, z + 1, x)))


def send_core(v):
    return lax.ppermute(v, "rep", [(i, i ^ 1) for i in range(8)])


def send_zhi_swap(v, d):
    return lax.ppermute(v, "rep", [(2 * h + c, (h ^ d) * 2 + c) for h in range(4) for c in range(2)])


def kernel_call(kernel, name, out_shape, limit, places, out_places, flops=0, scratch=(), aliases=None):
    spaces = {"v": pltpu.VMEM, "s": pltpu.SMEM, "a": pl.ANY, "h": pltpu.HBM}

    def call(*args):
        count = sum(math.prod(a.shape) * a.dtype.itemsize for a in (*args, *out_shape))
        return pl.pallas_call(
            kernel,
            out_shape=out_shape,
            in_specs=[pl.BlockSpec(memory_space=spaces[p]) for p in places],
            out_specs=[pl.BlockSpec(memory_space=spaces[p]) for p in out_places],
            scratch_shapes=list(scratch),
            input_output_aliases=aliases or {},
            compiler_params=pltpu.CompilerParams(vmem_limit_bytes=limit << 20),
            cost_estimate=pl.CostEstimate(flops=flops, bytes_accessed=2 * count, transcendentals=0),
            name=name,
        )(*args)

    return call


def struct(shape, dtype=BF16):
    return jax.ShapeDtypeStruct(shape, dtype)


RUN = D // (NY * NZ)
CHUNKS = HALF // 256


def pack(out, runs, wide=None):
    for r, run in enumerate(runs):
        out[2 * r] = run[:, :256].astype(BF16)
        out[2 * r + 1] = run[:, 256:512].astype(BF16)
    out[8] = jnp.concatenate([run[:, 512:] for run in runs], axis=1).astype(BF16)
    if wide is not None:
        for j in range(4):
            out[9 + j] = wide[:, j * 256 : j * 256 + 256].astype(BF16)


def unpack_run(ref, r):
    return jnp.concatenate(
        [ref[2 * r].astype(F32), ref[2 * r + 1].astype(F32), ref[8].astype(F32)[:, r * 64 : r * 64 + 64]],
        axis=1,
    )


def packed_rows(x, r, dx):
    col = lax.rem(x + dx, NX)
    first = r * 512 + col * ROWS
    second = jnp.where(col == NX - 1, 2048 + r * 64, first + 80)
    return pl.ds(pl.multiple_of(first, 16), 80), pl.ds(pl.multiple_of(second, 16), 64)


def sides_of(z, both):
    low, high = both[:, :RUN], both[:, RUN:]
    return jnp.where(z == 0, low, high), jnp.where(z == 0, high, low)


def run_span(y, r):
    return pl.ds(pl.multiple_of(lax.rem(y + r, NY) * (2 * RUN), 128), 2 * RUN)


def inverse_of(tok_ref):
    total = jnp.zeros((TOK, 128), F32)
    for k in range(D // 128):
        part = tok_ref[:, k * 128 : (k + 1) * 128].astype(F32)
        total = total + part * part
    return lax.rsqrt(jnp.sum(total, axis=1, keepdims=True) * (1.0 / D) + 1e-06)


def norm_kernel(where_ref, tok_any, scale_any, cot_any, keep_ref, give_ref, tok, scale, cot, sems):
    y, z = where_ref[0], where_ref[1]
    copies = [
        pltpu.make_async_copy(tok_any.at[:, pl.ds(k * 1152, 1152)], tok.at[:, pl.ds(k * 1152, 1152)], sems.at[k])
        for k in range(4)
    ]
    copies += [
        pltpu.make_async_copy(scale_any, scale, sems.at[4]),
        pltpu.make_async_copy(cot_any, cot, sems.at[5]),
    ]
    for copy in copies:
        copy.start()
    total = jnp.zeros((TOK, 128), F32)
    for k in range(D // 128):
        if k % 9 == 0:
            copies[k // 9].wait()
        part = tok[:, k * 128 : (k + 1) * 128].astype(F32)
        total = total + part * part
    inverse = lax.rsqrt(jnp.sum(total, axis=1, keepdims=True) * (1.0 / D) + 1e-06)
    for copy in copies[4:]:
        copy.wait()
    keep, give = [], []
    for r in range(NY):
        at = run_span(y, r)
        mine, other = sides_of(z, tok[:, at].astype(F32) * inverse * scale[:, at])
        keep.append(mine)
        give.append(other)
    pack(give_ref, give, cot[...])
    pack(keep_ref, keep)


PART, PACK = struct((CHUNKS, TOK, 256)), struct((CHUNKS + 4, TOK, 256))
norm_runs = kernel_call(
    norm_kernel,
    "norm",
    [PART, PACK],
    56,
    "saaa",
    "vv",
    scratch=[
        pltpu.VMEM((TOK, D), BF16),
        pltpu.VMEM((1, D), F32),
        pltpu.VMEM((TOK, HV), BF16),
        pltpu.SemaphoreType.DMA((6,)),
    ],
)


FOUR = struct((4, ROWS, 512))


def grad_kernel(where_ref, *refs):
    arrays, outs, (keep, got, cot, held, in_sems, sems) = refs[:3], refs[3:11], refs[11:]
    x = where_ref[2]
    run_all(
        [
            pltpu.make_async_copy(a, b, in_sems.at[i])
            for i, (a, b) in enumerate(zip(arrays, (keep, got, cot)))
        ]
    )

    def chunk(c):
        mine_t = keep[c].astype(F32).T.astype(BF16)
        other_t = got[c].astype(F32).T.astype(BF16)
        for j in range(4):
            cols = slice(j * 256, j * 256 + 256)
            part = jnp.dot(mine_t, cot[:, cols], preferred_element_type=F32)
            part = part + jnp.dot(other_t, got[9 + j], preferred_element_type=F32)
            held[c * 256 : c * 256 + 256, cols] = part.astype(BF16)

    chunk(8)
    copies = []
    for r in (2, 1, 3, 0):
        chunk(2 * r)
        chunk(2 * r + 1)
        for dx in range(NX):
            for half in range(2):
                out = outs[r].at[dx] if half == 0 else outs[4 + dx].at[r]
                for rows, to in zip(packed_rows(x, r, dx), (pl.ds(0, 80), pl.ds(80, 64))):
                    copy = pltpu.make_async_copy(
                        held.at[rows, pl.ds(half * 512, 512)], out.at[to], sems.at[len(copies)]
                    )
                    copy.start()
                    copies.append(copy)
    for copy in copies:
        copy.wait()


def run_all(copies):
    for copy in copies:
        copy.start()
    for copy in copies:
        copy.wait()


grad_terms = kernel_call(
    grad_kernel,
    "weight_terms",
    [FOUR] * 8,
    14,
    "saaa",
    "a" * 8,
    flops=2 * HALF * 2 * TOK * HV,
    scratch=[
        pltpu.VMEM(PART.shape, BF16),
        pltpu.VMEM(PACK.shape, BF16),
        pltpu.VMEM((TOK, HV), BF16),
        pltpu.VMEM((HALF, HV), BF16),
        pltpu.SemaphoreType.DMA((3,)),
        pltpu.SemaphoreType.DMA((64,)),
    ],
)


def near_kernel(*refs):
    parts, outs, sems = refs[:8], refs[8:10], refs[10]
    run_all(
        [
            pltpu.make_async_copy(parts[i], outs[i // 4].at[i % 4], sems.at[i])
            for i in range(8)
        ]
    )


make_near = kernel_call(
    near_kernel, "near", [FOUR] * 2, 4, "a" * 8, "aa", scratch=[pltpu.SemaphoreType.DMA((8,))]
)


def middle_kernel(*refs):
    outs, (own, others, sems) = refs[8:16], refs[16:]
    copies = []
    for half in range(2):
        terms = refs[half * 4 : half * 4 + 4]
        for i in (1, 3, 2, 0):
            total = terms[0][i].astype(F32)
            for term in terms[1:]:
                total = total + term[i].astype(F32)
            held = own.at[half] if i == 0 else others.at[half, i - 1]
            held[...] = total.astype(held.dtype)
            copy = pltpu.make_async_copy(held, outs[half * 4 + i], sems.at[half * 4 + i])
            copy.start()
            copies.append(copy)
    for copy in copies:
        copy.wait()


BLOCK = struct((ROWS, 512))
add_ring = kernel_call(
    middle_kernel,
    "add_ring",
    [struct((ROWS, 512), F32), BLOCK, BLOCK, BLOCK] * 2,
    8,
    "v" * 8,
    "a" * 8,
    scratch=[
        pltpu.VMEM((2, ROWS, 512), F32),
        pltpu.VMEM((2, 3, ROWS, 512), BF16),
        pltpu.SemaphoreType.DMA((8,)),
    ],
)
FACTOR = 1.0 / math.sqrt(8192)


def final_kernel(weight_ref, *refs):
    grad_ref, dots_ref = refs[8:]
    dots = jnp.zeros((ROWS, 1), F32)
    for half in range(2):
        own, one, two, three = refs[half * 4 : half * 4 + 4]
        total = own[...] + one[...].astype(F32) + two[...].astype(F32) + three[...].astype(F32)
        total = total * FACTOR
        cols = slice(half * 512, half * 512 + 512)
        grad_ref[:, cols] = total
        dots = dots + jnp.sum(total * weight_ref[:, cols].astype(F32), axis=1, keepdims=True)
    dots_ref[...] = dots


finish_grad = kernel_call(
    final_kernel,
    "finish",
    [struct((ROWS, HV), F32), struct((ROWS, 1), F32)],
    8,
    "v" * 9,
    "vv",
)


def side_kernel(where_ref, scale_ref, cot_ref, runs_ref, *refs):
    packed = runs_ref.shape[0] > CHUNKS
    pieces, outs, (whole, line, sems) = refs[:8], refs[8:-3], refs[-3:]
    y, z, x = where_ref[0], where_ref[1], where_ref[2]
    copies = []
    for r in range(NY):
        for dx in range(NX):
            for half, ref in enumerate((pieces[r].at[dx], pieces[4 + dx].at[r])):
                for rows, of in zip(packed_rows(x, r, dx), (pl.ds(0, 80), pl.ds(80, 64))):
                    copy = pltpu.make_async_copy(
                        ref.at[of], whole.at[rows, pl.ds(half * 512, 512)], sems.at[len(copies)]
                    )
                    copy.start()
                    copies.append(copy)
    scales = [sides_of(z, scale_ref[:, run_span(y, r)])[0] for r in range(NY)]
    tails = jnp.concatenate([scale[:, 512:] for scale in scales], axis=1)
    for c in range(CHUNKS):
        line[:, c * 256 : c * 256 + 256] = runs_ref[c]
    if packed:
        cot = jnp.concatenate([cot_ref[CHUNKS + j] for j in range(4)], axis=1)
    else:
        cot = cot_ref[...]
    for c in range(CHUNKS):
        if c % 2 == 0 and c < 8:
            for copy in copies[8 * c : 8 * c + 16]:
                copy.wait()
        back = lax.dot_general(
            cot,
            whole[c * 256 : c * 256 + 256, :],
            (((1,), (1,)), ((), ())),
            preferred_element_type=F32,
        )
        scale = scales[c // 2][:, c % 2 * 256 : c % 2 * 256 + 256] if c < 8 else tails
        outs[0][c] = (back * scale).astype(outs[0].dtype)
    for j in range(4):
        cols = slice(j * 256, j * 256 + 256)
        part = jnp.dot(line[...], whole[:, cols], preferred_element_type=F32)
        if packed:
            outs[0][CHUNKS + j] = part.astype(BF16)
        else:
            outs[1][:, cols] = part


def side_step(name, out_shape, places):
    return kernel_call(
        side_kernel,
        name,
        out_shape,
        14,
        "svvv" + "a" * 8,
        places,
        flops=4 * TOK * HALF * HV,
        scratch=[
            pltpu.VMEM((HALF, HV), BF16),
            pltpu.VMEM((TOK, HALF), BF16),
            pltpu.SemaphoreType.DMA((64,)),
        ],
    )


partner_side = side_step("partner_side", [PACK], "v")
own_side = side_step("own_side", [struct(PART.shape, F32), struct((TOK, HV), F32)], "vv")


def join_kernel(
    where_ref, tok_ref, back_any, part_any, got_ref, val_ref, grad_ref, whole, back, part, sems
):
    y, z = where_ref[0], where_ref[1]
    copies = [
        pltpu.make_async_copy(back_any, back, sems.at[0]),
        pltpu.make_async_copy(part_any, part, sems.at[1]),
    ]
    for copy in copies:
        copy.start()
    inverse = inverse_of(tok_ref)
    for copy in copies:
        copy.wait()
    sums = jnp.zeros((TOK, 128), F32)
    for r in range(NY):
        mine, other = unpack_run(back, r), unpack_run(got_ref, r)
        low, high = jnp.where(z == 0, mine, other), jnp.where(z == 0, other, mine)
        at = run_span(y, r)
        both = jnp.concatenate([low, high], axis=1)
        whole[:, at] = both
        mixed = both * tok_ref[:, at].astype(F32)
        for k in range(9):
            sums = sums + mixed[:, k * 128 : k * 128 + 128]
    lean = inverse * inverse * (jnp.sum(sums, axis=1, keepdims=True) * (1.0 / D))
    for k in range(0, D, 512):
        at = slice(k, k + 512)
        grad = inverse * (whole[:, at] - tok_ref[:, at].astype(F32) * lean)
        grad_ref[:, at] = grad.astype(BF16)
    for j in range(4):
        cols = slice(j * 256, j * 256 + 256)
        val_ref[:, cols] = (part[:, cols] + got_ref[CHUNKS + j].astype(F32)).astype(BF16)


join_sides = kernel_call(
    join_kernel,
    "join_sides",
    [struct((TOK, HV)), struct((TOK, D))],
    24,
    "svaav",
    "vv",
    scratch=[
        pltpu.VMEM((TOK, D), F32),
        pltpu.VMEM(PART.shape, F32),
        pltpu.VMEM((TOK, HV), F32),
        pltpu.SemaphoreType.DMA((2,)),
    ],
)


def pick(stack, row_frag):
    return jnp.where(row_frag[:, None] == 1, stack[1], stack[0])


def outer_start(replica_weights, base, fragment):
    row_frag = jnp.repeat(fragment, 8)
    pseudo = (pick(replica_weights[0], row_frag).astype(F32) - pick(base, row_frag)).astype(BF16)
    core = lax.axis_index("rep") % 2
    keep = lax.dynamic_slice_in_dim(pseudo, core * 512, 512, 1)
    got = send_core(lax.dynamic_slice_in_dim(pseudo, (1 - core) * 512, 512, 1))
    return keep.astype(F32) + got.astype(F32)


def outer_end(total, base, momentum, fragment):
    row_frag = jnp.repeat(fragment, 8)
    core = lax.axis_index("rep") % 2
    mine = total / 8
    theirs = send_core(mine)
    delta = jnp.where(
        core == 0,
        jnp.concatenate([mine, theirs], axis=1),
        jnp.concatenate([theirs, mine], axis=1),
    )
    new_momentum = 0.9 * pick(momentum, row_frag) + delta
    new_base = pick(base, row_frag) + 0.7 * (delta + 0.9 * new_momentum)
    return new_base, new_momentum


def add_zhi(total, d):
    return total + send_zhi_swap(total.astype(BF16), d).astype(F32)


def sides(own, send):
    return send(own, -1), send(own, 1)


def around(own, send, near=None):
    right, left = near or sides(own, send)
    return [own, right, send(after(own, right), 2), left]


def collect(blocks, send):
    one, three = send(blocks[1], 1), send(blocks[3], -1)
    return [blocks[0], one, send(after(blocks[2], one), 2), three]


def per_device(
    tokens, norm_scale, value_weight, cotangent, replica_weights, base, momentum, fragment
):
    tokens, weight, cot = tokens[0], value_weight[0], cotangent[0]
    me = lax.axis_index("fsdp")
    where = jnp.stack([me // (NZ * NX), me // NX % NZ, me % NX]).astype(jnp.int32)
    rings = ((send_x, send_y), (send_y, send_x))

    own = [weight[:, half * 512 : half * 512 + 512] for half in range(2)]
    first_steps = [sides(own[half], rings[half][0]) for half in range(2)]
    keep, give = norm_runs(where, tokens, norm_scale, cot)
    got = send_z(give)
    pair_sum = outer_start(replica_weights, base, fragment)

    parts = []
    for half, (first, _) in enumerate(rings):
        parts += around(after(own[half], give, pair_sum), first, first_steps[half])
    near = make_near(*parts)
    pieces = []
    for n, (_, second) in zip(near, rings):
        pieces += around(n, second)

    terms = grad_terms(where, keep, got, cot)
    sums = []
    for half, (_, second) in enumerate(rings):
        sums += collect(terms[half * 4 : half * 4 + 4], second)
    total = add_zhi(add_zhi(after(pair_sum, got), 1), 2)

    late = after(got, terms[0])
    (packed,) = partner_side(where, norm_scale, late, late, *pieces)
    back = send_z(after(packed, total))
    own_back, own_values = own_side(where, norm_scale, after(cot, packed), keep, *pieces)

    sums = add_ring(*sums)
    last = []
    for half, (first, _) in enumerate(rings):
        last += collect(sums[half * 4 : half * 4 + 4], first)
    values, input_grad = join_sides(where, tokens, own_back, own_values, back)
    weight_grad, dots = finish_grad(after(weight, values), *last)
    scale_grad = dots[:, 0] / lax.dynamic_slice_in_dim(norm_scale[0], me * ROWS, ROWS)
    new_base, new_momentum = outer_end(after(total, own_back), base, momentum, fragment)
    return (
        values[None],
        input_grad[None],
        weight_grad[None],
        scale_grad[None],
        new_base,
        new_momentum,
    )


def solution(mesh):
    in_specs = (
        P("rep", "fsdp", None),
        P("rep", None),
        P("rep", "fsdp", None),
        P("rep", "fsdp", None),
        P("rep", None, "fsdp", None),
        P(None, "fsdp", None),
        P(None, "fsdp", None),
        P("fsdp"),
    )
    out_specs = (
        P("rep", "fsdp", None),
        P("rep", "fsdp", None),
        P("rep", "fsdp", None),
        P("rep", "fsdp"),
        P("fsdp", None),
        P("fsdp", None),
    )
    return jax.shard_map(
        per_device, mesh=mesh, in_specs=in_specs, out_specs=out_specs, check_vma=False
    )
```

```python
import functools
import math

import jax
import jax.numpy as jnp
from jax import lax
from jax.experimental import pallas as pl
from jax.experimental.pallas import tpu as pltpu
from jax.sharding import PartitionSpec as P

D = 4608
HV = 1024
ROWS = 144
HALF = D // 2
TOK = 256
NX, NY, NZ = 4, 4, 2
F32, BF16 = jnp.float32, jnp.bfloat16


def fsdp_perm(move):
    pairs = []
    for y in range(NY):
        for z in range(NZ):
            for x in range(NX):
                a, b, c = move(y, z, x)
                pairs.append(((y * NZ + z) * NX + x, (a % NY * NZ + b % NZ) * NX + c % NX))
    return pairs


def after(v, *others):
    return lax.optimization_barrier((v, *others))[0]


def send_x(v, d):
    return lax.ppermute(v, "fsdp", fsdp_perm(lambda y, z, x: (y, z, x + d)))


def send_y(v, d):
    return lax.ppermute(v, "fsdp", fsdp_perm(lambda y, z, x: (y + d, z, x)))


def send_z(v):
    return lax.ppermute(v, "fsdp", fsdp_perm(lambda y, z, x: (y, z + 1, x)))


def send_core(v):
    return lax.ppermute(v, "rep", [(i, i ^ 1) for i in range(8)])


def send_zhi_swap(v, d):
    return lax.ppermute(v, "rep", [(2 * h + c, (h ^ d) * 2 + c) for h in range(4) for c in range(2)])


def kernel_call(kernel, name, out_shape, limit, places, out_places, flops=0, scratch=(), aliases=None):
    spaces = {"v": pltpu.VMEM, "s": pltpu.SMEM, "a": pl.ANY, "h": pltpu.HBM}

    def call(*args):
        count = sum(math.prod(a.shape) * a.dtype.itemsize for a in (*args, *out_shape))
        return pl.pallas_call(
            kernel,
            out_shape=out_shape,
            in_specs=[pl.BlockSpec(memory_space=spaces[p]) for p in places],
            out_specs=[pl.BlockSpec(memory_space=spaces[p]) for p in out_places],
            scratch_shapes=list(scratch),
            input_output_aliases=aliases or {},
            compiler_params=pltpu.CompilerParams(vmem_limit_bytes=limit << 20),
            cost_estimate=pl.CostEstimate(flops=flops, bytes_accessed=2 * count, transcendentals=0),
            name=name,
        )(*args)

    return call


def struct(shape, dtype=BF16):
    return jax.ShapeDtypeStruct(shape, dtype)


RUN = D // (NY * NZ)
CHUNKS = HALF // 256


def pack(out, runs, wide=None):
    line = jnp.concatenate(runs, axis=1)
    for c in range(CHUNKS):
        out[c] = line[:, c * 256 : c * 256 + 256].astype(BF16)
    if wide is not None:
        for j in range(4):
            out[9 + j] = wide[:, j * 256 : j * 256 + 256].astype(BF16)


def unpack_run(ref, r):
    parts = []
    for c in range(r * RUN // 256, (r * RUN + RUN - 1) // 256 + 1):
        first, last = max(r * RUN - c * 256, 0), min(r * RUN + RUN - c * 256, 256)
        parts.append(ref[c][:, first:last])
    return jnp.concatenate(parts, axis=1)


def packed_rows(x, r, dx):
    return pl.ds(pl.multiple_of(r * RUN + lax.rem(x + dx, NX) * ROWS, 16), ROWS)


def sides_of(z, both):
    low, high = both[:, :RUN], both[:, RUN:]
    return jnp.where(z == 0, low, high), jnp.where(z == 0, high, low)


def run_span(y, r):
    return pl.ds(pl.multiple_of(lax.rem(y + r, NY) * (2 * RUN), 128), 2 * RUN)


def inverse_of(tok_ref):
    total = jnp.zeros((TOK, 128), F32)
    for k in range(D // 128):
        part = tok_ref[:, k * 128 : (k + 1) * 128].astype(F32)
        total = total + part * part
    return lax.rsqrt(jnp.sum(total, axis=1, keepdims=True) * (1.0 / D) + 1e-06)


def norm_kernel(where_ref, tok_any, scale_any, cot_any, keep_ref, give_ref, tok, scale, cot, sems):
    y, z = where_ref[0], where_ref[1]
    copies = [
        pltpu.make_async_copy(tok_any.at[:, pl.ds(k * 1152, 1152)], tok.at[:, pl.ds(k * 1152, 1152)], sems.at[k])
        for k in range(4)
    ]
    copies += [
        pltpu.make_async_copy(scale_any, scale, sems.at[4]),
        pltpu.make_async_copy(cot_any, cot, sems.at[5]),
    ]
    for copy in copies:
        copy.start()
    total = jnp.zeros((TOK, 128), F32)
    for k in range(D // 128):
        if k % 9 == 0:
            copies[k // 9].wait()
        part = tok[:, k * 128 : (k + 1) * 128].astype(F32)
        total = total + part * part
    inverse = lax.rsqrt(jnp.sum(total, axis=1, keepdims=True) * (1.0 / D) + 1e-06)
    for copy in copies[4:]:
        copy.wait()
    keep, give = [], []
    for r in range(NY):
        at = run_span(y, r)
        both = (tok[:, at].astype(F32) * inverse * scale[:, at]).astype(BF16)
        mine, other = sides_of(z, both)
        keep.append(mine)
        give.append(other)
    pack(give_ref, give, cot[...])
    pack(keep_ref, keep)


PART, PACK = struct((CHUNKS, TOK, 256)), struct((CHUNKS + 4, TOK, 256))
norm_runs = kernel_call(
    norm_kernel,
    "norm",
    [PART, PACK],
    56,
    "saaa",
    "vv",
    scratch=[
        pltpu.VMEM((TOK, D), BF16),
        pltpu.VMEM((1, D), F32),
        pltpu.VMEM((TOK, HV), BF16),
        pltpu.SemaphoreType.DMA((6,)),
    ],
)


FOUR = struct((4, ROWS, 512))


def grad_kernel(where_ref, *refs):
    arrays, outs, (keep, got, cot, held, in_sems, sems) = refs[:3], refs[3:11], refs[11:]
    x = where_ref[2]
    run_all(
        [
            pltpu.make_async_copy(a, b, in_sems.at[i])
            for i, (a, b) in enumerate(zip(arrays, (keep, got, cot)))
        ]
    )

    def chunk(c):
        mine_t = keep[c].astype(F32).T.astype(BF16)
        other_t = got[c].astype(F32).T.astype(BF16)
        for j in range(4):
            cols = slice(j * 256, j * 256 + 256)
            part = jnp.dot(mine_t, cot[:, cols], preferred_element_type=F32)
            part = part + jnp.dot(other_t, got[9 + j], preferred_element_type=F32)
            held[c * 256 : c * 256 + 256, cols] = part.astype(BF16)

    copies = []
    for c in range(CHUNKS):
        chunk(c)
        if c % 2 or c == 0:
            continue
        r = c // 2 - 1
        for dx in range(NX):
            for half in range(2):
                out = outs[r].at[dx] if half == 0 else outs[4 + dx].at[r]
                copy = pltpu.make_async_copy(
                    held.at[packed_rows(x, r, dx), pl.ds(half * 512, 512)], out, sems.at[len(copies)]
                )
                copy.start()
                copies.append(copy)
    for copy in copies:
        copy.wait()


def run_all(copies):
    for copy in copies:
        copy.start()
    for copy in copies:
        copy.wait()


grad_terms = kernel_call(
    grad_kernel,
    "weight_terms",
    [FOUR] * 8,
    14,
    "saaa",
    "a" * 8,
    flops=2 * HALF * 2 * TOK * HV,
    scratch=[
        pltpu.VMEM(PART.shape, BF16),
        pltpu.VMEM(PACK.shape, BF16),
        pltpu.VMEM((TOK, HV), BF16),
        pltpu.VMEM((HALF, HV), BF16),
        pltpu.SemaphoreType.DMA((3,)),
        pltpu.SemaphoreType.DMA((32,)),
    ],
)


def near_kernel(*refs):
    parts, outs, sems = refs[:8], refs[8:10], refs[10]
    run_all(
        [
            pltpu.make_async_copy(parts[i], outs[i // 4].at[i % 4], sems.at[i])
            for i in range(8)
        ]
    )


make_near = kernel_call(
    near_kernel, "near", [FOUR] * 2, 4, "a" * 8, "aa", scratch=[pltpu.SemaphoreType.DMA((8,))]
)


def middle_kernel(*refs):
    outs, (own, others, sems) = refs[8:16], refs[16:]
    copies = []
    for half in range(2):
        terms = refs[half * 4 : half * 4 + 4]
        for i in (1, 3, 2, 0):
            total = terms[0][i].astype(F32)
            for term in terms[1:]:
                total = total + term[i].astype(F32)
            held = own.at[half] if i == 0 else others.at[half, i - 1]
            held[...] = total.astype(held.dtype)
            copy = pltpu.make_async_copy(held, outs[half * 4 + i], sems.at[half * 4 + i])
            copy.start()
            copies.append(copy)
    for copy in copies:
        copy.wait()


BLOCK = struct((ROWS, 512))
add_ring = kernel_call(
    middle_kernel,
    "add_ring",
    [struct((ROWS, 512), F32), BLOCK, BLOCK, BLOCK] * 2,
    8,
    "v" * 8,
    "a" * 8,
    scratch=[
        pltpu.VMEM((2, ROWS, 512), F32),
        pltpu.VMEM((2, 3, ROWS, 512), BF16),
        pltpu.SemaphoreType.DMA((8,)),
    ],
)
FACTOR = 1.0 / math.sqrt(8192)


def final_kernel(weight_ref, *refs):
    grad_ref, dots_ref = refs[8:]
    dots = jnp.zeros((ROWS, 1), F32)
    for half in range(2):
        own, one, two, three = refs[half * 4 : half * 4 + 4]
        total = own[...] + one[...].astype(F32) + two[...].astype(F32) + three[...].astype(F32)
        total = total * FACTOR
        cols = slice(half * 512, half * 512 + 512)
        grad_ref[:, cols] = total
        dots = dots + jnp.sum(total * weight_ref[:, cols].astype(F32), axis=1, keepdims=True)
    dots_ref[...] = dots


finish_grad = kernel_call(
    final_kernel,
    "finish",
    [struct((ROWS, HV), F32), struct((ROWS, 1), F32)],
    8,
    "v" * 9,
    "vv",
)


def side_kernel(where_ref, scale_ref, cot_ref, runs_ref, *refs):
    packed = runs_ref.shape[0] > CHUNKS
    pieces, outs, (whole, line, sems) = refs[:8], refs[8:-3], refs[-3:]
    y, z, x = where_ref[0], where_ref[1], where_ref[2]
    copies = []
    for r in range(NY):
        for dx in range(NX):
            for half, ref in enumerate((pieces[r].at[dx], pieces[4 + dx].at[r])):
                copy = pltpu.make_async_copy(
                    ref,
                    whole.at[packed_rows(x, r, dx), pl.ds(half * 512, 512)],
                    sems.at[len(copies)],
                )
                copy.start()
                copies.append(copy)
    scales = [sides_of(z, scale_ref[:, run_span(y, r)])[0] for r in range(NY)]
    scales = jnp.concatenate(scales, axis=1)
    for c in range(CHUNKS):
        line[:, c * 256 : c * 256 + 256] = runs_ref[c]
    if packed:
        cot = jnp.concatenate([cot_ref[CHUNKS + j] for j in range(4)], axis=1)
    else:
        cot = cot_ref[...]
    for c in range(CHUNKS):
        if c % 2 == 0 and c < 8:
            for copy in copies[4 * c : 4 * c + 8]:
                copy.wait()
        back = lax.dot_general(
            cot,
            whole[c * 256 : c * 256 + 256, :],
            (((1,), (1,)), ((), ())),
            preferred_element_type=F32,
        )
        outs[0][c] = (back * scales[:, c * 256 : c * 256 + 256]).astype(outs[0].dtype)
    for j in range(4):
        cols = slice(j * 256, j * 256 + 256)
        part = jnp.dot(line[...], whole[:, cols], preferred_element_type=F32)
        if packed:
            outs[0][CHUNKS + j] = part.astype(BF16)
        else:
            outs[1][:, cols] = part


def side_step(name, out_shape, places):
    return kernel_call(
        side_kernel,
        name,
        out_shape,
        14,
        "svvv" + "a" * 8,
        places,
        flops=4 * TOK * HALF * HV,
        scratch=[
            pltpu.VMEM((HALF, HV), BF16),
            pltpu.VMEM((TOK, HALF), BF16),
            pltpu.SemaphoreType.DMA((32,)),
        ],
    )


partner_side = side_step("partner_side", [PACK], "v")
own_side = side_step("own_side", [struct(PART.shape, F32), struct((TOK, HV), F32)], "vv")


def join_kernel(
    where_ref, tok_ref, back_any, part_any, got_ref, val_ref, grad_ref, whole, back, part, sems
):
    y, z = where_ref[0], where_ref[1]
    copies = [
        pltpu.make_async_copy(back_any, back, sems.at[0]),
        pltpu.make_async_copy(part_any, part, sems.at[1]),
    ]
    for copy in copies:
        copy.start()
    inverse = inverse_of(tok_ref)
    for copy in copies:
        copy.wait()
    sums = jnp.zeros((TOK, 128), F32)
    for r in range(NY):
        mine, other = unpack_run(back, r), unpack_run(got_ref, r).astype(F32)
        low, high = jnp.where(z == 0, mine, other), jnp.where(z == 0, other, mine)
        at = run_span(y, r)
        both = jnp.concatenate([low, high], axis=1)
        whole[:, at] = both
        mixed = both * tok_ref[:, at].astype(F32)
        for k in range(9):
            sums = sums + mixed[:, k * 128 : k * 128 + 128]
    lean = inverse * inverse * (jnp.sum(sums, axis=1, keepdims=True) * (1.0 / D))
    for k in range(0, D, 512):
        at = slice(k, k + 512)
        grad = inverse * (whole[:, at] - tok_ref[:, at].astype(F32) * lean)
        grad_ref[:, at] = grad.astype(BF16)
    for j in range(4):
        cols = slice(j * 256, j * 256 + 256)
        val_ref[:, cols] = (part[:, cols] + got_ref[CHUNKS + j].astype(F32)).astype(BF16)


join_sides = kernel_call(
    join_kernel,
    "join_sides",
    [struct((TOK, HV)), struct((TOK, D))],
    24,
    "svaav",
    "vv",
    scratch=[
        pltpu.VMEM((TOK, D), F32),
        pltpu.VMEM(PART.shape, F32),
        pltpu.VMEM((TOK, HV), F32),
        pltpu.SemaphoreType.DMA((2,)),
    ],
)


def pick(stack, row_frag):
    return jnp.where(row_frag[:, None] == 1, stack[1], stack[0])


def outer_start(replica_weights, base, fragment):
    row_frag = jnp.repeat(fragment, 8)
    pseudo = (pick(replica_weights[0], row_frag).astype(F32) - pick(base, row_frag)).astype(BF16)
    core = lax.axis_index("rep") % 2
    keep = lax.dynamic_slice_in_dim(pseudo, core * 512, 512, 1)
    got = send_core(lax.dynamic_slice_in_dim(pseudo, (1 - core) * 512, 512, 1))
    return keep.astype(F32) + got.astype(F32)


def outer_end(total, base, momentum, fragment):
    row_frag = jnp.repeat(fragment, 8)
    core = lax.axis_index("rep") % 2
    mine = total / 8
    theirs = send_core(mine)
    delta = jnp.where(
        core == 0,
        jnp.concatenate([mine, theirs], axis=1),
        jnp.concatenate([theirs, mine], axis=1),
    )
    new_momentum = 0.9 * pick(momentum, row_frag) + delta
    new_base = pick(base, row_frag) + 0.7 * (delta + 0.9 * new_momentum)
    return new_base, new_momentum


def add_zhi(total, d):
    return total + send_zhi_swap(total.astype(BF16), d).astype(F32)


def sides(own, send):
    return send(own, -1), send(own, 1)


def around(own, send, near=None):
    right, left = near or sides(own, send)
    return [own, right, send(after(own, right), 2), left]


def collect(blocks, send):
    one, three = send(blocks[1], 1), send(blocks[3], -1)
    return [blocks[0], one, send(after(blocks[2], one), 2), three]


def per_device(
    tokens, norm_scale, value_weight, cotangent, replica_weights, base, momentum, fragment
):
    tokens, weight, cot = tokens[0], value_weight[0], cotangent[0]
    me = lax.axis_index("fsdp")
    where = jnp.stack([me // (NZ * NX), me // NX % NZ, me % NX]).astype(jnp.int32)
    rings = ((send_x, send_y), (send_y, send_x))

    own = [weight[:, half * 512 : half * 512 + 512] for half in range(2)]
    first_steps = [sides(own[half], rings[half][0]) for half in range(2)]
    keep, give = norm_runs(where, tokens, norm_scale, cot)
    got = send_z(give)
    pair_sum = outer_start(replica_weights, base, fragment)

    parts = []
    for half, (first, _) in enumerate(rings):
        parts += around(after(own[half], give, pair_sum), first, first_steps[half])
    near = make_near(*parts)
    pieces = []
    for n, (_, second) in zip(near, rings):
        pieces += around(n, second)

    terms = grad_terms(where, keep, got, cot)
    sums = []
    for half, (_, second) in enumerate(rings):
        sums += collect(terms[half * 4 : half * 4 + 4], second)
    total = add_zhi(add_zhi(after(pair_sum, got), 1), 2)

    late = after(got, terms[0])
    (packed,) = partner_side(where, norm_scale, late, late, *pieces)
    back = send_z(after(packed, total))
    own_back, own_values = own_side(where, norm_scale, after(cot, packed), keep, *pieces)

    sums = add_ring(*sums)
    last = []
    for half, (first, _) in enumerate(rings):
        last += collect(sums[half * 4 : half * 4 + 4], first)
    values, input_grad = join_sides(where, tokens, own_back, own_values, back)
    weight_grad, dots = finish_grad(after(weight, values), *last)
    scale_grad = dots[:, 0] / lax.dynamic_slice_in_dim(norm_scale[0], me * ROWS, ROWS)
    new_base, new_momentum = outer_end(after(total, own_back), base, momentum, fragment)
    return (
        values[None],
        input_grad[None],
        weight_grad[None],
        scale_grad[None],
        new_base,
        new_momentum,
    )


def solution(mesh):
    in_specs = (
        P("rep", "fsdp", None),
        P("rep", None),
        P("rep", "fsdp", None),
        P("rep", "fsdp", None),
        P("rep", None, "fsdp", None),
        P(None, "fsdp", None),
        P(None, "fsdp", None),
        P("fsdp"),
    )
    out_specs = (
        P("rep", "fsdp", None),
        P("rep", "fsdp", None),
        P("rep", "fsdp", None),
        P("rep", "fsdp"),
        P("fsdp", None),
        P("fsdp", None),
    )
    return jax.shard_map(
        per_device, mesh=mesh, in_specs=in_specs, out_specs=out_specs, check_vma=False
    )
```

```python
import functools
import math

import jax
import jax.numpy as jnp
from jax import lax
from jax.experimental import pallas as pl
from jax.experimental.pallas import tpu as pltpu
from jax.sharding import PartitionSpec as P

D = 4608
HV = 1024
ROWS = 144
HALF = D // 2
TOK = 256
NX, NY, NZ = 4, 4, 2
F32, BF16 = jnp.float32, jnp.bfloat16


def fsdp_perm(move):
    pairs = []
    for y in range(NY):
        for z in range(NZ):
            for x in range(NX):
                a, b, c = move(y, z, x)
                pairs.append(((y * NZ + z) * NX + x, (a % NY * NZ + b % NZ) * NX + c % NX))
    return pairs


def after(v, *others):
    return lax.optimization_barrier((v, *others))[0]


def send_x(v, d):
    return lax.ppermute(v, "fsdp", fsdp_perm(lambda y, z, x: (y, z, x + d)))


def send_y(v, d):
    return lax.ppermute(v, "fsdp", fsdp_perm(lambda y, z, x: (y + d, z, x)))


def send_z(v):
    return lax.ppermute(v, "fsdp", fsdp_perm(lambda y, z, x: (y, z + 1, x)))


def send_core(v):
    return lax.ppermute(v, "rep", [(i, i ^ 1) for i in range(8)])


def send_zhi_swap(v, d):
    return lax.ppermute(v, "rep", [(2 * h + c, (h ^ d) * 2 + c) for h in range(4) for c in range(2)])


def kernel_call(kernel, name, out_shape, limit, places, out_places, flops=0, scratch=(), aliases=None):
    spaces = {"v": pltpu.VMEM, "s": pltpu.SMEM, "a": pl.ANY, "h": pltpu.HBM}

    def call(*args):
        count = sum(math.prod(a.shape) * a.dtype.itemsize for a in (*args, *out_shape))
        return pl.pallas_call(
            kernel,
            out_shape=out_shape,
            in_specs=[pl.BlockSpec(memory_space=spaces[p]) for p in places],
            out_specs=[pl.BlockSpec(memory_space=spaces[p]) for p in out_places],
            scratch_shapes=list(scratch),
            input_output_aliases=aliases or {},
            compiler_params=pltpu.CompilerParams(vmem_limit_bytes=limit << 20),
            cost_estimate=pl.CostEstimate(flops=flops, bytes_accessed=2 * count, transcendentals=0),
            name=name,
        )(*args)

    return call


def struct(shape, dtype=BF16):
    return jax.ShapeDtypeStruct(shape, dtype)


RUN = D // (NY * NZ)
CHUNKS = HALF // 256


def pack(out, runs, wide=None):
    line = jnp.concatenate(runs, axis=1)
    for c in range(CHUNKS):
        out[c] = line[:, c * 256 : c * 256 + 256].astype(BF16)
    if wide is not None:
        for j in range(4):
            out[9 + j] = wide[:, j * 256 : j * 256 + 256].astype(BF16)


STEP = 64


def unpack_run(ref, r, at):
    parts = []
    for c in range(r * RUN // 256, (r * RUN + RUN - 1) // 256 + 1):
        first, last = max(r * RUN - c * 256, 0), min(r * RUN + RUN - c * 256, 256)
        parts.append(ref[c, at, :][:, first:last])
    return jnp.concatenate(parts, axis=1)


def packed_rows(x, r, dx):
    return pl.ds(pl.multiple_of(r * RUN + lax.rem(x + dx, NX) * ROWS, 16), ROWS)


def sides_of(z, both):
    low, high = both[:, :RUN], both[:, RUN:]
    return jnp.where(z == 0, low, high), jnp.where(z == 0, high, low)


def run_span(y, r):
    return pl.ds(pl.multiple_of(lax.rem(y + r, NY) * (2 * RUN), 128), 2 * RUN)


def inverse_of(tok_ref):
    total = jnp.zeros((TOK, 128), F32)
    for k in range(D // 128):
        part = tok_ref[:, k * 128 : (k + 1) * 128].astype(F32)
        total = total + part * part
    return lax.rsqrt(jnp.sum(total, axis=1, keepdims=True) * (1.0 / D) + 1e-06)


def norm_kernel(where_ref, tok_any, scale_any, cot_any, keep_ref, give_ref, tok, scale, cot, sems):
    y, z = where_ref[0], where_ref[1]
    copies = [
        pltpu.make_async_copy(tok_any.at[:, pl.ds(k * 1152, 1152)], tok.at[:, pl.ds(k * 1152, 1152)], sems.at[k])
        for k in range(4)
    ]
    copies += [
        pltpu.make_async_copy(scale_any, scale, sems.at[4]),
        pltpu.make_async_copy(cot_any, cot, sems.at[5]),
    ]
    for copy in copies:
        copy.start()
    total = jnp.zeros((TOK, 128), F32)
    for k in range(D // 128):
        if k % 9 == 0:
            copies[k // 9].wait()
        part = tok[:, k * 128 : (k + 1) * 128].astype(F32)
        total = total + part * part
    inverse = lax.rsqrt(jnp.sum(total, axis=1, keepdims=True) * (1.0 / D) + 1e-06)
    for copy in copies[4:]:
        copy.wait()
    keep, give = [], []
    for r in range(NY):
        at = run_span(y, r)
        both = (tok[:, at].astype(F32) * inverse * scale[:, at]).astype(BF16)
        mine, other = sides_of(z, both)
        keep.append(mine)
        give.append(other)
    pack(give_ref, give, cot[...])
    pack(keep_ref, keep)


PART, PACK = struct((CHUNKS, TOK, 256)), struct((CHUNKS + 4, TOK, 256))
norm_runs = kernel_call(
    norm_kernel,
    "norm",
    [PART, PACK],
    56,
    "saaa",
    "vv",
    scratch=[
        pltpu.VMEM((TOK, D), BF16),
        pltpu.VMEM((1, D), F32),
        pltpu.VMEM((TOK, HV), BF16),
        pltpu.SemaphoreType.DMA((6,)),
    ],
)


FOUR = struct((4, ROWS, 512))


def grad_kernel(where_ref, *refs):
    arrays, outs, (keep, got, cot, held, in_sems, sems) = refs[:3], refs[3:11], refs[11:]
    x = where_ref[2]
    run_all(
        [
            pltpu.make_async_copy(a, b, in_sems.at[i])
            for i, (a, b) in enumerate(zip(arrays, (keep, got, cot)))
        ]
    )

    def chunk(c):
        mine_t = keep[c].astype(F32).T.astype(BF16)
        other_t = got[c].astype(F32).T.astype(BF16)
        for j in range(4):
            cols = slice(j * 256, j * 256 + 256)
            part = jnp.dot(mine_t, cot[:, cols], preferred_element_type=F32)
            part = part + jnp.dot(other_t, got[9 + j], preferred_element_type=F32)
            held[c * 256 : c * 256 + 256, cols] = part.astype(BF16)

    copies = []
    for c in range(CHUNKS):
        chunk(c)
        if c % 2 or c == 0:
            continue
        r = c // 2 - 1
        for dx in range(NX):
            for half in range(2):
                out = outs[r].at[dx] if half == 0 else outs[4 + dx].at[r]
                copy = pltpu.make_async_copy(
                    held.at[packed_rows(x, r, dx), pl.ds(half * 512, 512)], out, sems.at[len(copies)]
                )
                copy.start()
                copies.append(copy)
    for copy in copies:
        copy.wait()


def run_all(copies):
    for copy in copies:
        copy.start()
    for copy in copies:
        copy.wait()


grad_terms = kernel_call(
    grad_kernel,
    "weight_terms",
    [FOUR] * 8,
    14,
    "saaa",
    "a" * 8,
    flops=2 * HALF * 2 * TOK * HV,
    scratch=[
        pltpu.VMEM(PART.shape, BF16),
        pltpu.VMEM(PACK.shape, BF16),
        pltpu.VMEM((TOK, HV), BF16),
        pltpu.VMEM((HALF, HV), BF16),
        pltpu.SemaphoreType.DMA((3,)),
        pltpu.SemaphoreType.DMA((32,)),
    ],
)


def near_kernel(*refs):
    parts, outs, sems = refs[:8], refs[8:10], refs[10]
    run_all(
        [
            pltpu.make_async_copy(parts[i], outs[i // 4].at[i % 4], sems.at[i])
            for i in range(8)
        ]
    )


make_near = kernel_call(
    near_kernel, "near", [FOUR] * 2, 4, "a" * 8, "aa", scratch=[pltpu.SemaphoreType.DMA((8,))]
)


def middle_kernel(*refs):
    outs, (own, others, sems) = refs[8:16], refs[16:]
    copies = []
    for half in range(2):
        terms = refs[half * 4 : half * 4 + 4]
        for i in (1, 3, 2, 0):
            total = terms[0][i].astype(F32)
            for term in terms[1:]:
                total = total + term[i].astype(F32)
            held = own.at[half] if i == 0 else others.at[half, i - 1]
            held[...] = total.astype(held.dtype)
            copy = pltpu.make_async_copy(held, outs[half * 4 + i], sems.at[half * 4 + i])
            copy.start()
            copies.append(copy)
    for copy in copies:
        copy.wait()


BLOCK = struct((ROWS, 512))
add_ring = kernel_call(
    middle_kernel,
    "add_ring",
    [struct((ROWS, 512), F32), BLOCK, BLOCK, BLOCK] * 2,
    8,
    "v" * 8,
    "a" * 8,
    scratch=[
        pltpu.VMEM((2, ROWS, 512), F32),
        pltpu.VMEM((2, 3, ROWS, 512), BF16),
        pltpu.SemaphoreType.DMA((8,)),
    ],
)
FACTOR = 1.0 / math.sqrt(8192)


def final_kernel(weight_ref, *refs):
    grad_ref, dots_ref = refs[8:]
    dots = jnp.zeros((ROWS, 1), F32)
    for half in range(2):
        own, one, two, three = refs[half * 4 : half * 4 + 4]
        total = own[...] + one[...].astype(F32) + two[...].astype(F32) + three[...].astype(F32)
        total = total * FACTOR
        cols = slice(half * 512, half * 512 + 512)
        grad_ref[:, cols] = total
        dots = dots + jnp.sum(total * weight_ref[:, cols].astype(F32), axis=1, keepdims=True)
    dots_ref[...] = dots


finish_grad = kernel_call(
    final_kernel,
    "finish",
    [struct((ROWS, HV), F32), struct((ROWS, 1), F32)],
    8,
    "v" * 9,
    "vv",
)


def side_kernel(where_ref, scale_ref, cot_ref, runs_ref, *refs):
    packed = runs_ref.shape[0] > CHUNKS
    pieces, outs, (whole, line, sems) = refs[:8], refs[8:-3], refs[-3:]
    y, z, x = where_ref[0], where_ref[1], where_ref[2]
    copies = []
    for r in range(NY):
        for dx in range(NX):
            for half, ref in enumerate((pieces[r].at[dx], pieces[4 + dx].at[r])):
                copy = pltpu.make_async_copy(
                    ref,
                    whole.at[packed_rows(x, r, dx), pl.ds(half * 512, 512)],
                    sems.at[len(copies)],
                )
                copy.start()
                copies.append(copy)
    scales = [sides_of(z, scale_ref[:, run_span(y, r)])[0] for r in range(NY)]
    scales = jnp.concatenate(scales, axis=1)
    for c in range(CHUNKS):
        line[:, c * 256 : c * 256 + 256] = runs_ref[c]
    if packed:
        cot = jnp.concatenate([cot_ref[CHUNKS + j] for j in range(4)], axis=1)
    else:
        cot = cot_ref[...]
    for c in range(CHUNKS):
        if c % 2 == 0 and c < 8:
            for copy in copies[4 * c : 4 * c + 8]:
                copy.wait()
        back = lax.dot_general(
            cot,
            whole[c * 256 : c * 256 + 256, :],
            (((1,), (1,)), ((), ())),
            preferred_element_type=F32,
        )
        outs[0][c] = (back * scales[:, c * 256 : c * 256 + 256]).astype(outs[0].dtype)
    for j in range(4):
        cols = slice(j * 256, j * 256 + 256)
        part = jnp.dot(line[...], whole[:, cols], preferred_element_type=F32)
        if packed:
            outs[0][CHUNKS + j] = part.astype(BF16)
        else:
            outs[1][:, cols] = part


def side_step(name, out_shape, places):
    return kernel_call(
        side_kernel,
        name,
        out_shape,
        14,
        "svvv" + "a" * 8,
        places,
        flops=4 * TOK * HALF * HV,
        scratch=[
            pltpu.VMEM((HALF, HV), BF16),
            pltpu.VMEM((TOK, HALF), BF16),
            pltpu.SemaphoreType.DMA((32,)),
        ],
    )


partner_side = side_step("partner_side", [PACK], "v")
own_side = side_step("own_side", [struct(PART.shape, F32), struct((TOK, HV), F32)], "vv")


def join_kernel(
    where_ref, tok_ref, back_any, part_any, got_ref, val_ref, grad_ref, whole, back, part, sems
):
    y, z = where_ref[0], where_ref[1]
    copies = [
        pltpu.make_async_copy(back_any, back, sems.at[0]),
        pltpu.make_async_copy(part_any, part, sems.at[1]),
    ]
    for copy in copies:
        copy.start()
    for copy in copies:
        copy.wait()

    def rows(i, _):
        at = pl.ds(pl.multiple_of(i * STEP, STEP), STEP)
        total = jnp.zeros((STEP, 128), F32)
        for k in range(D // 128):
            toks = tok_ref[at, k * 128 : (k + 1) * 128].astype(F32)
            total = total + toks * toks
        inverse = lax.rsqrt(jnp.sum(total, axis=1, keepdims=True) * (1.0 / D) + 1e-06)
        sums = jnp.zeros((STEP, 128), F32)
        for r in range(NY):
            mine, other = unpack_run(back, r, at), unpack_run(got_ref, r, at).astype(F32)
            low, high = jnp.where(z == 0, mine, other), jnp.where(z == 0, other, mine)
            span = run_span(y, r)
            both = jnp.concatenate([low, high], axis=1)
            whole[:, span] = both
            mixed = both * tok_ref[at, span].astype(F32)
            for k in range(9):
                sums = sums + mixed[:, k * 128 : k * 128 + 128]
        lean = inverse * inverse * (jnp.sum(sums, axis=1, keepdims=True) * (1.0 / D))
        for k in range(0, D, 512):
            cols = slice(k, k + 512)
            grad = inverse * (whole[:, cols] - tok_ref[at, cols].astype(F32) * lean)
            grad_ref[at, cols] = grad.astype(BF16)
        for j in range(4):
            cols = slice(j * 256, j * 256 + 256)
            val_ref[at, cols] = (part[at, cols] + got_ref[CHUNKS + j, at, :].astype(F32)).astype(BF16)
        return 0

    lax.fori_loop(0, TOK // STEP, rows, 0)


join_sides = kernel_call(
    join_kernel,
    "join_sides",
    [struct((TOK, HV)), struct((TOK, D))],
    24,
    "svaav",
    "vv",
    scratch=[
        pltpu.VMEM((STEP, D), F32),
        pltpu.VMEM(PART.shape, F32),
        pltpu.VMEM((TOK, HV), F32),
        pltpu.SemaphoreType.DMA((2,)),
    ],
)


def pick(stack, row_frag):
    return jnp.where(row_frag[:, None] == 1, stack[1], stack[0])


def outer_start(replica_weights, base, fragment):
    row_frag = jnp.repeat(fragment, 8)
    pseudo = (pick(replica_weights[0], row_frag).astype(F32) - pick(base, row_frag)).astype(BF16)
    core = lax.axis_index("rep") % 2
    keep = lax.dynamic_slice_in_dim(pseudo, core * 512, 512, 1)
    got = send_core(lax.dynamic_slice_in_dim(pseudo, (1 - core) * 512, 512, 1))
    return keep.astype(F32) + got.astype(F32)


def outer_end(total, base, momentum, fragment):
    row_frag = jnp.repeat(fragment, 8)
    core = lax.axis_index("rep") % 2
    mine = total / 8
    theirs = send_core(mine)
    delta = jnp.where(
        core == 0,
        jnp.concatenate([mine, theirs], axis=1),
        jnp.concatenate([theirs, mine], axis=1),
    )
    new_momentum = 0.9 * pick(momentum, row_frag) + delta
    new_base = pick(base, row_frag) + 0.7 * (delta + 0.9 * new_momentum)
    return new_base, new_momentum


def add_zhi(total, d):
    return total + send_zhi_swap(total.astype(BF16), d).astype(F32)


def sides(own, send):
    return send(own, -1), send(own, 1)


def around(own, send, near=None):
    right, left = near or sides(own, send)
    return [own, right, send(after(own, right), 2), left]


def collect(blocks, send):
    one, three = send(blocks[1], 1), send(blocks[3], -1)
    return [blocks[0], one, send(after(blocks[2], one), 2), three]


def per_device(
    tokens, norm_scale, value_weight, cotangent, replica_weights, base, momentum, fragment
):
    tokens, weight, cot = tokens[0], value_weight[0], cotangent[0]
    me = lax.axis_index("fsdp")
    where = jnp.stack([me // (NZ * NX), me // NX % NZ, me % NX]).astype(jnp.int32)
    rings = ((send_x, send_y), (send_y, send_x))

    own = [weight[:, half * 512 : half * 512 + 512] for half in range(2)]
    first_steps = [sides(own[half], rings[half][0]) for half in range(2)]
    keep, give = norm_runs(where, tokens, norm_scale, cot)
    got = send_z(give)
    pair_sum = outer_start(replica_weights, base, fragment)

    parts = []
    for half, (first, _) in enumerate(rings):
        parts += around(after(own[half], give, pair_sum), first, first_steps[half])
    near = make_near(*parts)
    pieces = []
    for n, (_, second) in zip(near, rings):
        pieces += around(n, second)

    terms = grad_terms(where, keep, got, cot)
    sums = []
    for half, (_, second) in enumerate(rings):
        sums += collect(terms[half * 4 : half * 4 + 4], second)
    total = add_zhi(add_zhi(after(pair_sum, got), 1), 2)

    late = after(got, terms[0])
    (packed,) = partner_side(where, norm_scale, late, late, *pieces)
    back = send_z(after(packed, total))
    own_back, own_values = own_side(where, norm_scale, after(cot, packed), keep, *pieces)

    sums = add_ring(*sums)
    last = []
    for half, (first, _) in enumerate(rings):
        last += collect(sums[half * 4 : half * 4 + 4], first)
    values, input_grad = join_sides(where, tokens, own_back, own_values, back)
    weight_grad, dots = finish_grad(after(weight, values), *last)
    scale_grad = dots[:, 0] / lax.dynamic_slice_in_dim(norm_scale[0], me * ROWS, ROWS)
    new_base, new_momentum = outer_end(after(total, own_back), base, momentum, fragment)
    return (
        values[None],
        input_grad[None],
        weight_grad[None],
        scale_grad[None],
        new_base,
        new_momentum,
    )


def solution(mesh):
    in_specs = (
        P("rep", "fsdp", None),
        P("rep", None),
        P("rep", "fsdp", None),
        P("rep", "fsdp", None),
        P("rep", None, "fsdp", None),
        P(None, "fsdp", None),
        P(None, "fsdp", None),
        P("fsdp"),
    )
    out_specs = (
        P("rep", "fsdp", None),
        P("rep", "fsdp", None),
        P("rep", "fsdp", None),
        P("rep", "fsdp"),
        P("fsdp", None),
        P("fsdp", None),
    )
    return jax.shard_map(
        per_device, mesh=mesh, in_specs=in_specs, out_specs=out_specs, check_vma=False
    )
```
